32 devices in a mesh: groups: 2 (over x), expert: 4 (over y, core), sub: 4 (over z).
Axes of the slice: x: 2, y: 2, z: 4, core: 2. Of those that a mesh axis runs over, the one named last changes fastest.
Arguments:
- residual: bfloat16 [256, 2048], P(('groups', 'expert', 'sub')), parts along dimension 0, may hold values from -6 to 6
- query: bfloat16 [256, 2048], P(('groups', 'expert', 'sub')), parts along dimension 0, may hold values from -5 to 5
- new_key: bfloat16 [256, 512], P(('groups', 'expert', 'sub')), parts along dimension 0, may hold values from -5 to 5
- new_value: bfloat16 [256, 512], P(('groups', 'expert', 'sub')), parts along dimension 0, may hold values from -6 to 6
- key_cache: bfloat16 [256, 128, 512], P(('groups', 'expert', 'sub')), parts along dimension 0, may hold values from -5 to 5
- value_cache: bfloat16 [256, 128, 512], P(('groups', 'expert', 'sub')), parts along dimension 0, may hold values from -6 to 6
- cache_len: int32 [256], P(('groups', 'expert', 'sub')), parts along dimension 0, may hold values from 1 to 128, as said below
- out_weight: bfloat16 [2048, 2048], P('sub'), may hold values from -0.125 to 0.125
- norm_gain: bfloat16 [2048], replicated, may hold values from 0.099609375 to 1.8984375
- expert_ids: int32 [256, 8], P(('groups', 'expert', 'sub')), parts along dimension 0, may hold values from 0 to 15, as said below
- gate_scores: float32 [256, 8], P(('groups', 'expert', 'sub')), parts along dimension 0, may hold values from 0.05 to 1
- expert_gate: bfloat16 [16, 2048, 768], P(('expert', 'sub')), may hold values from -0.125 to 0.125
- expert_up: bfloat16 [16, 2048, 768], P(('expert', 'sub')), may hold values from -0.125 to 0.125
- expert_down: bfloat16 [16, 768, 2048], P(('expert', 'sub')), may hold values from -0.21875 to 0.21875
Outputs:
- layer_out: bfloat16 [256, 2048], P(('groups', 'expert', 'sub')), parts along dimension 0
The draws below stay inside these ranges and needn't reach their ends.
There are 2 independent parts, one for each index of `groups`. The reference program is written for one: setup_inputs(seed, part) draws one part's arguments, and reference() takes and returns one part's arrays. A program takes and returns all parts, laid end to end along the dimension named above; an argument that names none is the same for every part. Nothing has to cross between parts.
Inputs may be any that keep to these rules, and one draw needn't show every extreme that they name: Stream t attends to cache positions below cache_len[t] and to its new frame; in every draw some stream holds all 128 frames. `expert_ids`: each row names 8 different experts. Among the 8 rows of one device no expert is named more than 8 times, and one expert is named exactly 8 times by the rows of every device.
All inputs are finite; a program needn't handle non-finite values.
Results may differ from the reference program's by a relative error of at most 0.0075.
Values may be sent and summed in bfloat16 or wider, within the bound.
No kernel may reach another device: no remote copies, remote signals or barrier semaphores. Data moves between devices by JAX's collectives and lax.ppermute only.
A program may use at most 64 MiB of HBM per device.

```python
import math
import jax
import jax.numpy as jnp
from jax import lax

D = 2048
HEADS = 16
KV_HEADS = 4
HEAD_DIM = 128
FF = 768
TOPK = 8
S_DEV = 8
CACHE = 128
EXPERTS = 16
TOKENS = 128
CAP = 8
N_EXPERT = 4
N_SUB = 4


def draw_query(key, part):
    key = jax.random.fold_in(key, 3)
    return jnp.clip(jax.random.normal(key, (TOKENS, HEADS * HEAD_DIM), jnp.float32), -5.0, 5.0).astype(jnp.bfloat16)


def draw_new_key(key, part):
    key = jax.random.fold_in(key, 4)
    return jnp.clip(jax.random.normal(key, (TOKENS, KV_HEADS * HEAD_DIM), jnp.float32), -5.0, 5.0).astype(jnp.bfloat16)


def draw_key_cache(key, part):
    key = jax.random.fold_in(key, 5)
    return jnp.clip(jax.random.normal(key, (TOKENS, CACHE, KV_HEADS * HEAD_DIM), jnp.float32), -5.0, 5.0).astype(jnp.bfloat16)


def draw_cache_len(key, part):
    key = jax.random.fold_in(key, 6)
    length_key, spot_key = jax.random.split(key, 2)
    lengths = jax.random.randint(length_key, (TOKENS,), 1, CACHE + 1)
    full_spot = jax.random.randint(spot_key, (), 0, TOKENS)
    return lengths.at[full_spot].set(CACHE).astype(jnp.int32)


def draw_expert_ids(key, part):
    key = jax.random.fold_in(key, 7)
    blocks = TOKENS // S_DEV
    per_group = S_DEV // CAP
    pop_key, noise_key, hot_key, row_key, col_key = jax.random.split(key, 5)
    popular = jax.random.randint(pop_key, (EXPERTS,), 0, 2 ** 21)
    hottest = jax.random.randint(hot_key, (), 0, EXPERTS)
    noise_level = jax.random.randint(noise_key, (blocks, CAP, EXPERTS), 0, 2 ** 20)
    labels = jnp.arange(EXPERTS, dtype=jnp.int32)
    scores = jnp.where(labels == hottest, 2 ** 23, noise_level + popular)
    scores = scores * EXPERTS + labels
    ranked = lax.top_k(scores, per_group * TOPK)[1]
    chosen_ids = ranked.reshape(blocks, S_DEV, TOPK)
    row_scores = jax.random.randint(row_key, (blocks, S_DEV), 0, 2 ** 20) * S_DEV + jnp.arange(S_DEV, dtype=jnp.int32)
    row_order = jnp.argsort(row_scores, axis=1, stable=True)
    chosen_ids = jnp.take_along_axis(chosen_ids, row_order[:, :, None], axis=1)
    col_scores = jax.random.randint(col_key, (blocks, S_DEV, TOPK), 0, 2 ** 20) * TOPK + jnp.arange(TOPK, dtype=jnp.int32)
    col_order = jnp.argsort(col_scores, axis=2, stable=True)
    chosen_ids = jnp.take_along_axis(chosen_ids, col_order, axis=2)
    return chosen_ids.reshape(TOKENS, TOPK).astype(jnp.int32)


def block_levels(rng, shape, cuts, low, largest):
    factor_of, own = 1.0, jax.random.fold_in(rng, 6)
    for dim, parts in cuts:
        heights = jnp.exp(jax.random.uniform(jax.random.fold_in(own, dim), (parts,), jnp.float32, low / len(cuts), largest / len(cuts)))
        factor_of = factor_of * jnp.repeat(heights, shape[dim] // parts).reshape([-1 if axis == dim else 1 for axis in range(len(shape))])
    return factor_of


def bell_draw(rng, dims, deviation, limit, cuts=(), kind=jnp.bfloat16):
    result = jax.random.normal(rng, dims, jnp.float32) * deviation
    if len(cuts) > 0:
        result = block_levels(rng, dims, cuts, -0.22, 0.18) * result
    return jnp.clip(result, min=-limit, max=limit).astype(kind)


def setup_inputs(seed: int = 0, part: int = 0) -> dict:
    key_list = jax.random.split(jax.random.key(seed), 15)
    part_keys = jax.random.split(jax.random.fold_in(key_list[14], part), 15)
    return {
        "residual": bell_draw(part_keys[0], (TOKENS, D), 1.0, 6.0, ((0, 16),)),
        "query": draw_query(jax.random.fold_in(jax.random.fold_in(key_list[14], part), 71), part),
        "new_key": draw_new_key(jax.random.fold_in(jax.random.fold_in(key_list[14], part), 71), part),
        "new_value": bell_draw(part_keys[3], (TOKENS, KV_HEADS * HEAD_DIM), 1.0, 6.0, ((0, 16),)),
        "key_cache": draw_key_cache(jax.random.fold_in(jax.random.fold_in(key_list[14], part), 71), part),
        "value_cache": bell_draw(part_keys[5], (TOKENS, CACHE, KV_HEADS * HEAD_DIM), 1.0, 6.0, ((0, 16),)),
        "cache_len": draw_cache_len(jax.random.fold_in(jax.random.fold_in(key_list[14], part), 71), part),
        "out_weight": bell_draw(key_list[7], (HEADS * HEAD_DIM, D), (HEADS * HEAD_DIM) ** -0.5, 0.125, ((0, 4),)),
        "norm_gain": jnp.clip(1.0 + 0.18 * jax.random.normal(key_list[8], (D,), jnp.float32), 0.099609375, 1.8984375).astype(jnp.bfloat16),
        "expert_ids": draw_expert_ids(jax.random.fold_in(jax.random.fold_in(key_list[14], part), 71), part),
        "gate_scores": jnp.clip(jnp.exp(math.log(1.0) - 2.9957323 * jax.random.uniform(part_keys[10], (TOKENS, TOPK), jnp.float32) ** block_levels(part_keys[10], (TOKENS, TOPK), ((0, 16),), -0.2, 0.2)), 0.05, 1.0),
        "expert_gate": bell_draw(key_list[11], (EXPERTS, D, FF), D ** -0.5, 0.125, ((0, 16),)),
        "expert_up": bell_draw(key_list[12], (EXPERTS, D, FF), D ** -0.5, 0.125, ((0, 16),)),
        "expert_down": bell_draw(key_list[13], (EXPERTS, FF, D), FF ** -0.5, 0.21875, ((0, 16),)),
    }


def reference(residual, query, new_key, new_value, key_cache, value_cache, cache_len, out_weight, norm_gain, expert_ids, gate_scores, expert_gate, expert_up, expert_down):
    streams = residual.shape[0]
    group_size = HEADS // KV_HEADS
    scale_factor = 1.0 / math.sqrt(HEAD_DIM)
    queries = query.astype(jnp.float32).reshape(streams, KV_HEADS, group_size, HEAD_DIM)
    keys_old = key_cache.astype(jnp.float32).reshape(streams, CACHE, KV_HEADS, HEAD_DIM)
    values_old = value_cache.astype(jnp.float32).reshape(streams, CACHE, KV_HEADS, HEAD_DIM)
    keys_new = new_key.astype(jnp.float32).reshape(streams, KV_HEADS, HEAD_DIM)
    values_new = new_value.astype(jnp.float32).reshape(streams, KV_HEADS, HEAD_DIM)
    scores_old = jnp.einsum('skgd,slkd->skgl', queries, keys_old) * scale_factor
    scores_new = jnp.einsum('skgd,skd->skg', queries, keys_new) * scale_factor
    is_valid = jnp.arange(CACHE, dtype=jnp.int32)[None, :] < cache_len[:, None]
    scores_old = jnp.where(is_valid[:, None, None, :], scores_old, -1e+30)
    highest = jnp.maximum(lax.optimization_barrier(jnp.max(scores_old, axis=3)), scores_new)
    exp_old = jnp.exp(scores_old - highest[..., None])
    exp_new = jnp.exp(scores_new - highest)
    total_mass = lax.optimization_barrier(jnp.sum(exp_old, axis=3)) + exp_new
    probs_old = (exp_old / total_mass[..., None]).astype(jnp.bfloat16)
    probs_new = (exp_new / total_mass).astype(jnp.bfloat16)
    context = jnp.einsum('skgl,slkd->skgd', probs_old.astype(jnp.float32), values_old)
    context = context + probs_new.astype(jnp.float32)[..., None] * values_new[:, :, None, :]
    context = context.reshape(streams, HEADS * HEAD_DIM).astype(jnp.bfloat16)
    hidden = residual.astype(jnp.float32) + jnp.dot(context, out_weight, preferred_element_type=jnp.float32)
    normed = hidden * lax.rsqrt(lax.optimization_barrier(jnp.mean(hidden * hidden, axis=1, keepdims=True)) + 1e-06)
    normed = (normed * norm_gain.astype(jnp.float32)).astype(jnp.bfloat16)
    flat_ids = expert_ids.reshape(-1).astype(jnp.int32)
    slot_total = streams * TOPK
    most_rows = CAP * N_EXPERT * N_SUB

    def one_expert(outputs, expert):
        picked = jnp.nonzero(flat_ids == expert, size=most_rows, fill_value=slot_total)[0].astype(jnp.int32)
        source_rows = normed[jnp.minimum(picked, slot_total - 1) // TOPK]
        gate_part = jnp.dot(source_rows, expert_gate[expert], preferred_element_type=jnp.float32)
        up_part = jnp.dot(source_rows, expert_up[expert], preferred_element_type=jnp.float32)
        activated = (jax.nn.silu(gate_part) * up_part).astype(jnp.bfloat16)
        produced = jnp.dot(activated, expert_down[expert], preferred_element_type=jnp.float32).astype(jnp.bfloat16)
        outputs = outputs.at[picked].set(produced, mode='drop')
        return (outputs, None)
    expert_out = lax.scan(one_expert, jnp.zeros((slot_total, D), jnp.bfloat16), jnp.arange(EXPERTS, dtype=jnp.int32))[0]
    weights = gate_scores / lax.optimization_barrier(jnp.sum(gate_scores, axis=1, keepdims=True))
    mixture = lax.optimization_barrier(jnp.sum(weights[:, :, None] * expert_out.astype(jnp.float32).reshape(streams, TOPK, D), axis=1))
    return (hidden + mixture).astype(jnp.bfloat16)
```

```python
import functools
import math

import jax
import jax.numpy as jnp
from jax import lax
from jax.experimental import pallas as pl
from jax.experimental.pallas import tpu as pltpu
from jax.sharding import PartitionSpec as P

HEAD_DIM = 128
LANES = 128
BF16, F32 = jnp.bfloat16, jnp.float32
VMEM = pl.BlockSpec(memory_space=pltpu.VMEM)
SMEM = pl.BlockSpec(memory_space=pltpu.SMEM)
ANY = pl.BlockSpec(memory_space=pl.ANY)


def params(mib):
    return pltpu.CompilerParams(vmem_limit_bytes=mib * 2**20)


def attend_kernel(len_ref, q_ref, nk_ref, nv_ref, k_hbm, v_hbm, out_ref, k_buf, v_buf, sems):
    k_copy = pltpu.make_async_copy(k_hbm, k_buf, sems.at[0])
    v_copy = pltpu.make_async_copy(v_hbm, v_buf, sems.at[1])
    k_copy.start()
    v_copy.start()
    streams, frames, kv_width = k_buf.shape
    heads = q_ref.shape[1] // HEAD_DIM
    group = heads // (kv_width // HEAD_DIM)
    scale = 1.0 / math.sqrt(HEAD_DIM)
    query = q_ref[...].astype(F32)
    new_key = nk_ref[...].astype(F32)
    zero = jnp.zeros((streams, HEAD_DIM), F32)
    rows, new_scores = [], []
    for h in range(heads):
        g = h // group
        q = query[:, h * HEAD_DIM : (h + 1) * HEAD_DIM]
        rows.append(
            jnp.concatenate([q if b == g else zero for b in range(kv_width // HEAD_DIM)], axis=1)
        )
        k = new_key[:, g * HEAD_DIM : (g + 1) * HEAD_DIM]
        new_scores.append(jnp.sum(q * k, axis=1, keepdims=True) * scale)
    spread = jnp.concatenate(rows, axis=0).astype(BF16)
    row = lax.broadcasted_iota(jnp.int32, (streams, streams * frames), 0)
    col = lax.broadcasted_iota(jnp.int32, (streams, streams * frames), 1)
    end = jnp.zeros_like(row)
    for s in range(streams):
        end = jnp.where(row == s, len_ref[s] + s * frames, end)
    valid = (col >= row * frames) & (col < end)
    k_copy.wait()
    scores = lax.dot_general(
        spread,
        k_buf[...].reshape(streams * frames, kv_width),
        (((1,), (1,)), ((), ())),
        preferred_element_type=F32,
    )
    probs, new_probs = [], []
    for h in range(heads):
        old = jnp.where(valid, scores[h * streams : (h + 1) * streams] * scale, -1e30)
        new = new_scores[h]
        top = jnp.maximum(jnp.max(old, axis=1, keepdims=True), new)
        old = jnp.exp(old - top)
        new = jnp.exp(new - top)
        total = jnp.sum(old, axis=1, keepdims=True) + new
        probs.append(old / total)
        new_probs.append((new / total).astype(BF16).astype(F32))
    probs = jnp.concatenate(probs, axis=0).astype(BF16)
    v_copy.wait()
    context = jnp.dot(
        probs, v_buf[...].reshape(streams * frames, kv_width), preferred_element_type=F32
    )
    new_value = nv_ref[...].astype(F32)
    width = out_ref.shape[2]
    for h in range(heads):
        c = (h // group) * HEAD_DIM
        part = context[h * streams : (h + 1) * streams, c : c + HEAD_DIM]
        part = part + new_probs[h] * new_value[:, c : c + HEAD_DIM]
        at = h * HEAD_DIM
        out_ref[at // width, :, at % width : at % width + HEAD_DIM] = part.astype(BF16)


def project_kernel(x_ref, w_ref, out_ref):
    pieces, streams, depth = x_ref.shape
    x = x_ref[...].astype(F32).reshape(pieces * streams, depth).astype(BF16)
    y = jnp.dot(x, w_ref[...], preferred_element_type=F32)
    out_ref[...] = y.reshape(pieces, streams, y.shape[1]).astype(BF16)


def norm_kernel(experts, part_ref, res_ref, gain_ref, ids_ref, gates_ref, hidden_ref, out_ref):
    hidden = res_ref[...].astype(F32)
    for i in range(part_ref.shape[0]):
        hidden = hidden + part_ref[i].astype(F32)
    hidden_ref[...] = hidden
    width = hidden.shape[1]
    normed = hidden * lax.rsqrt(jnp.mean(hidden * hidden, axis=1, keepdims=True) + 1e-06)
    normed = (normed * gain_ref[...].astype(F32)).astype(BF16)
    gates = gates_ref[...]
    weights = gates / jnp.sum(gates, axis=1, keepdims=True)
    ids = ids_ref[...]
    lane = lax.broadcasted_iota(jnp.int32, (ids.shape[0], out_ref.shape[2] - width), 1)
    label = jnp.where(lane >= experts, lane - experts, lane)
    table = jnp.zeros(lane.shape, F32)
    for k in range(ids.shape[1]):
        table = table + jnp.where(label == ids[:, k : k + 1], weights[:, k : k + 1], 0.0)
    high = table.astype(BF16)
    low = (table - high.astype(F32)).astype(BF16)
    table = jnp.where(lane < experts, high.astype(F32), low.astype(F32)).astype(BF16)
    for i in range(out_ref.shape[0]):
        out_ref[i, :, :width] = normed
        out_ref[i, :, width:] = table


def expert_kernel(experts, me_ref, own_ref, other_ref, gate_ref, up_ref, down_ref, keep_ref, send_ref):
    chips, streams, _ = own_ref.shape
    width = down_ref.shape[1]
    half = chips * streams

    def load(ref):
        return ref[...].astype(F32).reshape(half, ref.shape[2])

    full = jnp.concatenate([load(own_ref), load(other_ref)], axis=0)
    rows = full[:, :width].astype(BF16)
    table = full[:, width:]
    lane = lax.broadcasted_iota(jnp.int32, table.shape, 1)
    mine = me_ref[0]
    chosen = (lane == mine) | (lane == mine + experts)
    weight = jnp.sum(jnp.where(chosen, table, 0.0), axis=1, keepdims=True)
    gate = jnp.dot(rows, gate_ref[...], preferred_element_type=F32)
    up = jnp.dot(rows, up_ref[...], preferred_element_type=F32)
    act = (gate / (1.0 + jnp.exp(-gate)) * up).astype(BF16)
    y = jnp.dot(act, down_ref[...], preferred_element_type=F32) * weight
    keep_ref[...] = y[:half]
    send_ref[...] = y[half:].astype(BF16)


def body(
    residual,
    query,
    new_key,
    new_value,
    key_cache,
    value_cache,
    cache_len,
    out_weight,
    norm_gain,
    expert_ids,
    gate_scores,
    expert_gate,
    expert_up,
    expert_down,
):
    streams, width = residual.shape
    n_expert, n_sub = lax.axis_size("expert"), lax.axis_size("sub")
    experts = n_expert * n_sub
    chips = experts // 2
    both = ("expert", "sub")
    same_core = [
        [(2 * i + core) * n_sub + s for i in range(n_expert // 2) for s in range(n_sub)]
        for core in range(2)
    ]
    twins = [(i, i ^ 1) for i in range(n_expert)]
    shape = jax.ShapeDtypeStruct

    context = pl.pallas_call(
        attend_kernel,
        out_shape=shape((n_sub, streams, width // n_sub), BF16),
        in_specs=[SMEM, VMEM, VMEM, VMEM, ANY, ANY],
        out_specs=VMEM,
        scratch_shapes=[
            pltpu.VMEM(key_cache.shape, BF16),
            pltpu.VMEM(value_cache.shape, BF16),
            pltpu.SemaphoreType.DMA((2,)),
        ],
        compiler_params=params(16),
        name="attend",
    )(cache_len, query, new_key, new_value, key_cache, value_cache)
    context = lax.all_to_all(context, "sub", split_axis=0, concat_axis=0, tiled=True)

    partial = pl.pallas_call(
        project_kernel,
        out_shape=shape((n_sub, streams, width), BF16),
        in_specs=[VMEM, VMEM],
        out_specs=VMEM,
        compiler_params=params(16),
        name="project",
    )(context, out_weight)
    partial = lax.all_to_all(partial, "sub", split_axis=0, concat_axis=0, tiled=True)

    table = -(-2 * experts // LANES) * LANES
    hidden, rows = pl.pallas_call(
        functools.partial(norm_kernel, experts),
        out_shape=(shape((streams, width), F32), shape((chips, streams, width + table), BF16)),
        in_specs=[VMEM] * 5,
        out_specs=(VMEM, VMEM),
        compiler_params=params(16),
        name="norm",
    )(partial, residual, norm_gain.reshape(1, width), expert_ids, gate_scores)
    own = lax.all_to_all(
        rows, both, split_axis=0, concat_axis=0, tiled=True, axis_index_groups=same_core
    )
    other = lax.ppermute(own, "expert", twins)

    me = (lax.axis_index("expert") * n_sub + lax.axis_index("sub")).reshape(1)
    half = chips * streams
    keep, send = pl.pallas_call(
        functools.partial(expert_kernel, experts),
        out_shape=(shape((half, width), F32), shape((half, width), BF16)),
        in_specs=[SMEM] + [VMEM] * 5,
        out_specs=(VMEM, VMEM),
        compiler_params=params(48),
        name="expert",
    )(me, own, other, expert_gate[0], expert_up[0], expert_down[0])
    got = lax.ppermute(send, "expert", twins)
    summed = (keep + got.astype(F32)).astype(BF16).reshape(chips, streams, width)
    back = lax.all_to_all(
        summed, both, split_axis=0, concat_axis=0, tiled=True, axis_index_groups=same_core
    )
    return (hidden + jnp.sum(back.astype(F32), axis=0)).astype(BF16)


def solution(mesh):
    rows = P(("groups", "expert", "sub"), None)
    cache = P(("groups", "expert", "sub"), None, None)
    weights = P(("expert", "sub"), None, None)
    return jax.shard_map(
        body,
        mesh=mesh,
        in_specs=(
            rows,
            rows,
            rows,
            rows,
            cache,
            cache,
            P(("groups", "expert", "sub")),
            P("sub", None),
            P(),
            rows,
            rows,
            weights,
            weights,
            weights,
        ),
        out_specs=rows,
        check_vma=False,
    )
```

```python
import functools
import math

import jax
import jax.numpy as jnp
from jax import lax
from jax.experimental import pallas as pl
from jax.experimental.pallas import tpu as pltpu
from jax.sharding import PartitionSpec as P

HEAD_DIM = 128
LANES = 128
BF16, F32 = jnp.bfloat16, jnp.float32
VMEM = pl.BlockSpec(memory_space=pltpu.VMEM)
SMEM = pl.BlockSpec(memory_space=pltpu.SMEM)
HBM = pl.BlockSpec(memory_space=pltpu.HBM)
def params(mib):
    return pltpu.CompilerParams(vmem_limit_bytes=mib * 2**20)


def in_hbm(x):
    return pltpu.with_memory_space_constraint(x, pltpu.HBM)


def attend_kernel(
    experts,
    len_hbm,
    q_hbm,
    nk_hbm,
    nv_hbm,
    k_hbm,
    v_hbm,
    res_hbm,
    ids_hbm,
    gates_hbm,
    out_ref,
    res_ref,
    table_ref,
    len_ref,
    q_ref,
    nk_ref,
    nv_ref,
    k_buf,
    v_buf,
    ids_ref,
    gates_ref,
    sems,
):
    pairs = (
        (k_hbm, k_buf),
        (q_hbm, q_ref),
        (nk_hbm, nk_ref),
        (len_hbm, len_ref),
        (v_hbm, v_buf),
        (nv_hbm, nv_ref),
        (ids_hbm, ids_ref),
        (gates_hbm, gates_ref),
        (res_hbm, res_ref),
    )
    copies = [pltpu.make_async_copy(a, b, sems.at[i]) for i, (a, b) in enumerate(pairs)]
    for copy in copies:
        copy.start()
    for copy in copies[1:4]:
        copy.wait()
    streams, frames, kv_width = k_buf.shape
    heads = q_ref.shape[1] // HEAD_DIM
    group = heads // (kv_width // HEAD_DIM)
    scale = 1.0 / math.sqrt(HEAD_DIM)
    query = q_ref[...].astype(F32)
    new_key = nk_ref[...].astype(F32)
    zero = jnp.zeros((streams, HEAD_DIM), F32)
    rows, new_scores = [], []
    for h in range(heads):
        g = h // group
        q = query[:, h * HEAD_DIM : (h + 1) * HEAD_DIM]
        rows.append(
            jnp.concatenate([q if b == g else zero for b in range(kv_width // HEAD_DIM)], axis=1)
        )
        k = new_key[:, g * HEAD_DIM : (g + 1) * HEAD_DIM]
        new_scores.append(jnp.sum(q * k, axis=1, keepdims=True) * scale)
    spread = jnp.concatenate(rows, axis=0).astype(BF16)
    row = lax.broadcasted_iota(jnp.int32, (streams, streams * frames), 0)
    col = lax.broadcasted_iota(jnp.int32, (streams, streams * frames), 1)
    end = jnp.zeros_like(row)
    for s in range(streams):
        end = jnp.where(row == s, len_ref[s] + s * frames, end)
    valid = (col >= row * frames) & (col < end)
    copies[0].wait()
    scores = lax.dot_general(
        spread,
        k_buf[...].reshape(streams * frames, kv_width),
        (((1,), (1,)), ((), ())),
        preferred_element_type=F32,
    )
    probs, new_probs = [], []
    for h in range(heads):
        old = jnp.where(valid, scores[h * streams : (h + 1) * streams] * scale, -1e30)
        new = new_scores[h]
        top = jnp.maximum(jnp.max(old, axis=1, keepdims=True), new)
        old = jnp.exp(old - top)
        new = jnp.exp(new - top)
        total = jnp.sum(old, axis=1, keepdims=True) + new
        probs.append(old / total)
        new_probs.append((new / total).astype(BF16).astype(F32))
    probs = jnp.concatenate(probs, axis=0).astype(BF16)
    copies[4].wait()
    copies[5].wait()
    context = jnp.dot(
        probs, v_buf[...].reshape(streams * frames, kv_width), preferred_element_type=F32
    )
    new_value = nv_ref[...].astype(F32)
    width = out_ref.shape[2]
    for h in range(heads):
        c = (h // group) * HEAD_DIM
        part = context[h * streams : (h + 1) * streams, c : c + HEAD_DIM]
        part = part + new_probs[h] * new_value[:, c : c + HEAD_DIM]
        at = h * HEAD_DIM
        out_ref[at // width, :, at % width : at % width + HEAD_DIM] = part.astype(BF16)
    for copy in copies[6:]:
        copy.wait()
    gates = gates_ref[...]
    weights = gates / jnp.sum(gates, axis=1, keepdims=True)
    ids = ids_ref[...]
    lane = lax.broadcasted_iota(jnp.int32, table_ref.shape, 1)
    label = jnp.where(lane >= experts, lane - experts, lane)
    table = jnp.zeros(lane.shape, F32)
    for k in range(ids.shape[1]):
        table = table + jnp.where(label == ids[:, k : k + 1], weights[:, k : k + 1], 0.0)
    high = table.astype(BF16).astype(F32)
    table_ref[...] = jnp.where(lane < experts, high, table - high).astype(BF16)


def project_kernel(x_ref, w_ref, out_ref):
    pieces, streams, depth = x_ref.shape
    x = x_ref[...].astype(F32).reshape(pieces * streams, depth).astype(BF16)
    y = jnp.dot(x, w_ref[...], preferred_element_type=F32)
    out_ref[...] = y.reshape(pieces, streams, y.shape[1]).astype(BF16)


def norm_kernel(part_ref, res_ref, gain_ref, table_ref, hidden_ref, out_ref):
    hidden = res_ref[...].astype(F32)
    for i in range(part_ref.shape[0]):
        hidden = hidden + part_ref[i].astype(F32)
    hidden_ref[...] = hidden
    width = hidden.shape[1]
    normed = hidden * lax.rsqrt(jnp.mean(hidden * hidden, axis=1, keepdims=True) + 1e-06)
    normed = (normed * gain_ref[...].astype(F32)).astype(BF16)
    table = table_ref[...]
    for i in range(out_ref.shape[0]):
        out_ref[i, :, :width] = normed
        out_ref[i, :, width:] = table


def expert_kernel(
    experts,
    me_ref,
    own_ref,
    other_ref,
    gate_ref,
    up_hbm,
    down_hbm,
    keep_ref,
    send_ref,
    up_ref,
    down_ref,
    sems,
):
    up_copy = pltpu.make_async_copy(up_hbm, up_ref, sems.at[0])
    down_copy = pltpu.make_async_copy(down_hbm, down_ref, sems.at[1])
    up_copy.start()
    down_copy.start()
    chips, streams, _ = own_ref.shape
    width = down_ref.shape[1]
    half = chips * streams

    def load(ref):
        return ref[...].astype(F32).reshape(half, ref.shape[2])

    full = jnp.concatenate([load(own_ref), load(other_ref)], axis=0)
    rows = full[:, :width].astype(BF16)
    table = full[:, width:]
    lane = lax.broadcasted_iota(jnp.int32, table.shape, 1)
    mine = me_ref[0]
    chosen = (lane == mine) | (lane == mine + experts)
    weight = jnp.sum(jnp.where(chosen, table, 0.0), axis=1, keepdims=True)
    gate = jnp.dot(rows, gate_ref[...], preferred_element_type=F32)
    act = gate / (1.0 + jnp.exp(-gate))
    up_copy.wait()
    up = jnp.dot(rows, up_ref[...], preferred_element_type=F32)
    act = (act * up).astype(BF16)
    down_copy.wait()
    y = jnp.dot(act, down_ref[...], preferred_element_type=F32) * weight
    keep_ref[...] = y[:half]
    send_ref[...] = y[half:].astype(BF16)


def body(
    residual,
    query,
    new_key,
    new_value,
    key_cache,
    value_cache,
    cache_len,
    out_weight,
    norm_gain,
    expert_ids,
    gate_scores,
    expert_gate,
    expert_up,
    expert_down,
):
    streams, width = residual.shape
    n_expert, n_sub = lax.axis_size("expert"), lax.axis_size("sub")
    experts = n_expert * n_sub
    chips = experts // 2
    both = ("expert", "sub")
    same_core = [
        [(2 * i + core) * n_sub + s for i in range(n_expert // 2) for s in range(n_sub)]
        for core in range(2)
    ]
    twins = [(i, i ^ 1) for i in range(n_expert)]
    shape = jax.ShapeDtypeStruct

    table_width = -(-2 * experts // LANES) * LANES
    context, resident, table = pl.pallas_call(
        functools.partial(attend_kernel, experts),
        out_shape=(
            shape((n_sub, streams, width // n_sub), BF16),
            shape(residual.shape, BF16),
            shape((streams, table_width), BF16),
        ),
        in_specs=[HBM] * 9,
        out_specs=(VMEM, VMEM, VMEM),
        scratch_shapes=[
            pltpu.SMEM(cache_len.shape, jnp.int32),
            pltpu.VMEM(query.shape, BF16),
            pltpu.VMEM(new_key.shape, BF16),
            pltpu.VMEM(new_value.shape, BF16),
            pltpu.VMEM(key_cache.shape, BF16),
            pltpu.VMEM(value_cache.shape, BF16),
            pltpu.VMEM(expert_ids.shape, jnp.int32),
            pltpu.VMEM(gate_scores.shape, F32),
            pltpu.SemaphoreType.DMA((9,)),
        ],
        compiler_params=params(12),
        name="attend",
    )(
        *(
            in_hbm(a)
            for a in (
                cache_len,
                query,
                new_key,
                new_value,
                key_cache,
                value_cache,
                residual,
                expert_ids,
                gate_scores,
            )
        )
    )
    gate = expert_gate[0]
    context = lax.all_to_all(context, "sub", split_axis=0, concat_axis=0, tiled=True)

    partial = pl.pallas_call(
        project_kernel,
        out_shape=shape((n_sub, streams, width), BF16),
        in_specs=[VMEM, VMEM],
        out_specs=VMEM,
        compiler_params=params(8),
        name="project",
    )(context, out_weight)
    partial = lax.all_to_all(partial, "sub", split_axis=0, concat_axis=0, tiled=True)

    hidden, rows = pl.pallas_call(
        norm_kernel,
        out_shape=(shape((streams, width), F32), shape((chips, streams, width + table_width), BF16)),
        in_specs=[VMEM] * 4,
        out_specs=(VMEM, VMEM),
        compiler_params=params(8),
        name="norm",
    )(partial, resident, norm_gain.reshape(1, width), table)
    own = lax.all_to_all(
        rows, both, split_axis=0, concat_axis=0, tiled=True, axis_index_groups=same_core
    )
    other = lax.ppermute(own, "expert", twins)

    me = (lax.axis_index("expert") * n_sub + lax.axis_index("sub")).reshape(1)
    half = chips * streams
    keep, send = pl.pallas_call(
        functools.partial(expert_kernel, experts),
        out_shape=(shape((half, width), F32), shape((half, width), BF16)),
        in_specs=[SMEM, VMEM, VMEM, VMEM, HBM, HBM],
        out_specs=(VMEM, VMEM),
        scratch_shapes=[
            pltpu.VMEM(expert_up.shape[1:], BF16),
            pltpu.VMEM(expert_down.shape[1:], BF16),
            pltpu.SemaphoreType.DMA((2,)),
        ],
        compiler_params=params(18 + half // 16),
        name="expert",
    )(me, own, other, gate, in_hbm(expert_up[0]), in_hbm(expert_down[0]))
    got = lax.ppermute(send, "expert", twins)
    summed = (keep + got.astype(F32)).astype(BF16).reshape(chips, streams, width)
    back = lax.all_to_all(
        summed, both, split_axis=0, concat_axis=0, tiled=True, axis_index_groups=same_core
    )
    return (hidden + jnp.sum(back.astype(F32), axis=0)).astype(BF16)


def solution(mesh):
    rows = P(("groups", "expert", "sub"), None)
    cache = P(("groups", "expert", "sub"), None, None)
    weights = P(("expert", "sub"), None, None)
    return jax.shard_map(
        body,
        mesh=mesh,
        in_specs=(
            rows,
            rows,
            rows,
            rows,
            cache,
            cache,
            P(("groups", "expert", "sub")),
            P("sub", None),
            P(),
            rows,
            rows,
            weights,
            weights,
            weights,
        ),
        out_specs=rows,
        check_vma=False,
    )
```

```python
import functools
import math

import jax
import jax.numpy as jnp
from jax import lax
from jax.experimental import pallas as pl
from jax.experimental.pallas import tpu as pltpu
from jax.sharding import PartitionSpec as P

HEAD_DIM = 128
LANES = 128
BF16, F32 = jnp.bfloat16, jnp.float32
VMEM = pl.BlockSpec(memory_space=pltpu.VMEM)
SMEM = pl.BlockSpec(memory_space=pltpu.SMEM)
HBM = pl.BlockSpec(memory_space=pltpu.HBM)
def params(mib):
    return pltpu.CompilerParams(vmem_limit_bytes=mib * 2**20)


def in_hbm(x):
    return pltpu.with_memory_space_constraint(x, pltpu.HBM)


def in_vmem(x):
    return pltpu.with_memory_space_constraint(x, pltpu.VMEM)


def attend_kernel(
    experts,
    len_hbm,
    q_hbm,
    nk_hbm,
    nv_hbm,
    k_hbm,
    v_hbm,
    res_hbm,
    ids_hbm,
    gates_hbm,
    out_ref,
    res_ref,
    table_ref,
    len_ref,
    q_ref,
    nk_ref,
    nv_ref,
    k_buf,
    v_buf,
    ids_ref,
    gates_ref,
    sems,
):
    pairs = (
        (k_hbm, k_buf),
        (q_hbm, q_ref),
        (nk_hbm, nk_ref),
        (len_hbm, len_ref),
        (v_hbm, v_buf),
        (nv_hbm, nv_ref),
        (ids_hbm, ids_ref),
        (gates_hbm, gates_ref),
        (res_hbm, res_ref),
    )
    copies = [pltpu.make_async_copy(a, b, sems.at[i]) for i, (a, b) in enumerate(pairs)]
    for copy in copies:
        copy.start()
    for copy in copies[1:4]:
        copy.wait()
    streams, frames, kv_width = k_buf.shape
    heads = q_ref.shape[1] // HEAD_DIM
    group = heads // (kv_width // HEAD_DIM)
    scale = 1.0 / math.sqrt(HEAD_DIM)
    query = q_ref[...].astype(F32)
    new_key = nk_ref[...].astype(F32)
    zero = jnp.zeros((streams, HEAD_DIM), F32)
    rows, new_scores = [], []
    for h in range(heads):
        g = h // group
        q = query[:, h * HEAD_DIM : (h + 1) * HEAD_DIM]
        rows.append(
            jnp.concatenate([q if b == g else zero for b in range(kv_width // HEAD_DIM)], axis=1)
        )
        k = new_key[:, g * HEAD_DIM : (g + 1) * HEAD_DIM]
        new_scores.append(jnp.sum(q * k, axis=1, keepdims=True) * scale)
    spread = jnp.concatenate(rows, axis=0).astype(BF16)
    row = lax.broadcasted_iota(jnp.int32, (streams, streams * frames), 0)
    col = lax.broadcasted_iota(jnp.int32, (streams, streams * frames), 1)
    end = jnp.zeros_like(row)
    for s in range(streams):
        end = jnp.where(row == s, len_ref[s] + s * frames, end)
    valid = (col >= row * frames) & (col < end)
    copies[0].wait()
    scores = lax.dot_general(
        spread,
        k_buf[...].reshape(streams * frames, kv_width),
        (((1,), (1,)), ((), ())),
        preferred_element_type=F32,
    )
    probs, new_probs = [], []
    for h in range(heads):
        old = jnp.where(valid, scores[h * streams : (h + 1) * streams] * scale, -1e30)
        new = new_scores[h]
        top = jnp.maximum(jnp.max(old, axis=1, keepdims=True), new)
        old = jnp.exp(old - top)
        new = jnp.exp(new - top)
        total = jnp.sum(old, axis=1, keepdims=True) + new
        probs.append(old / total)
        new_probs.append((new / total).astype(BF16).astype(F32))
    probs = jnp.concatenate(probs, axis=0).astype(BF16)
    copies[4].wait()
    copies[5].wait()
    context = jnp.dot(
        probs, v_buf[...].reshape(streams * frames, kv_width), preferred_element_type=F32
    )
    new_value = nv_ref[...].astype(F32)
    width = out_ref.shape[2]
    for h in range(heads):
        c = (h // group) * HEAD_DIM
        part = context[h * streams : (h + 1) * streams, c : c + HEAD_DIM]
        part = part + new_probs[h] * new_value[:, c : c + HEAD_DIM]
        at = h * HEAD_DIM
        out_ref[at // width, :, at % width : at % width + HEAD_DIM] = part.astype(BF16)
    for copy in copies[6:]:
        copy.wait()
    gates = gates_ref[...]
    weights = gates / jnp.sum(gates, axis=1, keepdims=True)
    ids = ids_ref[...]
    lane = lax.broadcasted_iota(jnp.int32, table_ref.shape, 1)
    label = jnp.where(lane >= experts, lane - experts, lane)
    table = jnp.zeros(lane.shape, F32)
    for k in range(ids.shape[1]):
        table = table + jnp.where(label == ids[:, k : k + 1], weights[:, k : k + 1], 0.0)
    high = table.astype(BF16).astype(F32)
    table_ref[...] = jnp.where(lane < experts, high, table - high).astype(BF16)


def project_kernel(x_ref, w_ref, out_ref):
    pieces, streams, depth = x_ref.shape
    x = x_ref[...].astype(F32).reshape(pieces * streams, depth).astype(BF16)
    y = jnp.dot(x, w_ref[...], preferred_element_type=F32)
    out_ref[...] = y.reshape(pieces, streams, y.shape[1]).astype(BF16)


def norm_kernel(part_ref, res_ref, gain_ref, table_ref, _up, _down, hidden_ref, out_ref):
    hidden = res_ref[...].astype(F32)
    for i in range(part_ref.shape[0]):
        hidden = hidden + part_ref[i].astype(F32)
    hidden_ref[...] = hidden
    width = hidden.shape[1]
    normed = hidden * lax.rsqrt(jnp.mean(hidden * hidden, axis=1, keepdims=True) + 1e-06)
    normed = (normed * gain_ref[...].astype(F32).reshape(1, width)).astype(BF16)
    table = table_ref[...]
    for i in range(out_ref.shape[0]):
        out_ref[i, :, :width] = normed
        out_ref[i, :, width:] = table


def expert_kernel(
    experts,
    own_ref,
    other_ref,
    gate_ref,
    up_ref,
    down_ref,
    keep_ref,
    send_ref,
):
    chips, streams, _ = own_ref.shape
    width = down_ref.shape[1]
    half = chips * streams

    def load(ref):
        return ref[...].astype(F32).reshape(half, ref.shape[2])

    full = jnp.concatenate([load(own_ref), load(other_ref)], axis=0)
    rows = full[:, :width].astype(BF16)
    table = full[:, width:]
    lane = lax.broadcasted_iota(jnp.int32, table.shape, 1)
    mine = lax.axis_index("expert") * lax.axis_size("sub") + lax.axis_index("sub")
    chosen = (lane == mine) | (lane == mine + experts)
    weight = jnp.sum(jnp.where(chosen, table, 0.0), axis=1, keepdims=True)
    gate = jnp.dot(rows, gate_ref[...], preferred_element_type=F32)
    act = gate / (1.0 + jnp.exp(-gate))
    up = jnp.dot(rows, up_ref[...], preferred_element_type=F32)
    act = (act * up).astype(BF16)
    y = jnp.dot(act, down_ref[...], preferred_element_type=F32) * weight
    keep_ref[...] = y[:half]
    send_ref[...] = y[half:].astype(BF16)


def body(
    residual,
    query,
    new_key,
    new_value,
    key_cache,
    value_cache,
    cache_len,
    out_weight,
    norm_gain,
    expert_ids,
    gate_scores,
    expert_gate,
    expert_up,
    expert_down,
):
    streams, width = residual.shape
    n_expert, n_sub = lax.axis_size("expert"), lax.axis_size("sub")
    experts = n_expert * n_sub
    chips = experts // 2
    both = ("expert", "sub")
    same_core = [
        [(2 * i + core) * n_sub + s for i in range(n_expert // 2) for s in range(n_sub)]
        for core in range(2)
    ]
    twins = [(i, i ^ 1) for i in range(n_expert)]
    shape = jax.ShapeDtypeStruct

    table_width = -(-2 * experts // LANES) * LANES
    context, resident, table = pl.pallas_call(
        functools.partial(attend_kernel, experts),
        out_shape=(
            shape((n_sub, streams, width // n_sub), BF16),
            shape(residual.shape, BF16),
            shape((streams, table_width), BF16),
        ),
        in_specs=[HBM] * 9,
        out_specs=(VMEM, VMEM, VMEM),
        scratch_shapes=[
            pltpu.SMEM(cache_len.shape, jnp.int32),
            pltpu.VMEM(query.shape, BF16),
            pltpu.VMEM(new_key.shape, BF16),
            pltpu.VMEM(new_value.shape, BF16),
            pltpu.VMEM(key_cache.shape, BF16),
            pltpu.VMEM(value_cache.shape, BF16),
            pltpu.VMEM(expert_ids.shape, jnp.int32),
            pltpu.VMEM(gate_scores.shape, F32),
            pltpu.SemaphoreType.DMA((9,)),
        ],
        compiler_params=params(12),
        name="attend",
    )(
        *(
            in_hbm(a)
            for a in (
                cache_len,
                query,
                new_key,
                new_value,
                key_cache,
                value_cache,
                residual,
                expert_ids,
                gate_scores,
            )
        )
    )
    gate = expert_gate[0]
    context = lax.all_to_all(context, "sub", split_axis=0, concat_axis=0, tiled=True)

    partial = pl.pallas_call(
        project_kernel,
        out_shape=shape((n_sub, streams, width), BF16),
        in_specs=[VMEM, VMEM],
        out_specs=VMEM,
        compiler_params=params(8),
        name="project",
    )(context, out_weight)
    partial = lax.all_to_all(partial, "sub", split_axis=0, concat_axis=0, tiled=True)

    hidden, rows = pl.pallas_call(
        norm_kernel,
        out_shape=(shape((streams, width), F32), shape((chips, streams, width + table_width), BF16)),
        in_specs=[VMEM] * 4 + [HBM] * 2,
        out_specs=(VMEM, VMEM),
        compiler_params=params(8),
        name="norm",
    )(partial, resident, norm_gain, table, in_hbm(expert_up[0]), in_hbm(expert_down[0]))
    own = lax.all_to_all(
        rows, both, split_axis=0, concat_axis=0, tiled=True, axis_index_groups=same_core
    )
    other = lax.ppermute(own, "expert", twins)

    half = chips * streams
    keep, send = pl.pallas_call(
        functools.partial(expert_kernel, experts),
        out_shape=(shape((half, width), F32), shape((half, width), BF16)),
        in_specs=[VMEM] * 5,
        out_specs=(VMEM, VMEM),
        compiler_params=params(18 + half // 16),
        name="expert",
    )(own, other, in_vmem(gate), in_vmem(expert_up[0]), in_vmem(expert_down[0]))
    got = lax.ppermute(send, "expert", twins)
    summed = (keep + got.astype(F32)).astype(BF16).reshape(chips, streams, width)
    back = lax.all_to_all(
        summed, both, split_axis=0, concat_axis=0, tiled=True, axis_index_groups=same_core
    )
    return (hidden + jnp.sum(back.astype(F32), axis=0)).astype(BF16)


def solution(mesh):
    rows = P(("groups", "expert", "sub"), None)
    cache = P(("groups", "expert", "sub"), None, None)
    weights = P(("expert", "sub"), None, None)
    return jax.shard_map(
        body,
        mesh=mesh,
        in_specs=(
            rows,
            rows,
            rows,
            rows,
            cache,
            cache,
            P(("groups", "expert", "sub")),
            P("sub", None),
            P(),
            rows,
            rows,
            weights,
            weights,
            weights,
        ),
        out_specs=rows,
        check_vma=False,
    )
```

```python
import functools
import math

import jax
import jax.numpy as jnp
from jax import lax
from jax.experimental import pallas as pl
from jax.experimental.pallas import tpu as pltpu
from jax.sharding import PartitionSpec as P

HEAD_DIM = 128
LANES = 128
BF16, F32 = jnp.bfloat16, jnp.float32
VMEM = pl.BlockSpec(memory_space=pltpu.VMEM)
SMEM = pl.BlockSpec(memory_space=pltpu.SMEM)
HBM = pl.BlockSpec(memory_space=pltpu.HBM)
def params(mib):
    return pltpu.CompilerParams(vmem_limit_bytes=mib * 2**20)


def in_hbm(x):
    return pltpu.with_memory_space_constraint(x, pltpu.HBM)


def in_vmem(x):
    return pltpu.with_memory_space_constraint(x, pltpu.VMEM)


def attend_kernel(
    experts,
    steps,
    len_hbm,
    q_hbm,
    nk_hbm,
    nv_hbm,
    k_hbm,
    v_hbm,
    res_hbm,
    ids_hbm,
    gates_hbm,
    weight_hbm,
    gain_hbm,
    *refs,
):
    out_refs = refs[: len(steps)]
    (
    res_ref,
    table_ref,
    weight_ref,
    gain_ref,
    ctx_ref,
    len_ref,
    q_ref,
    nk_ref,
    nv_ref,
    k_buf,
    v_buf,
    ids_ref,
    gates_ref,
    sems,
    ) = refs[len(steps) :]
    pairs = (
        (k_hbm, k_buf),
        (q_hbm, q_ref),
        (nk_hbm, nk_ref),
        (len_hbm, len_ref),
        (v_hbm, v_buf),
        (nv_hbm, nv_ref),
        (ids_hbm, ids_ref),
        (gates_hbm, gates_ref),
        (res_hbm, res_ref),
        (weight_hbm, weight_ref),
        (gain_hbm, gain_ref),
    )
    copies = [pltpu.make_async_copy(a, b, sems.at[i]) for i, (a, b) in enumerate(pairs)]
    for copy in copies:
        copy.start()
    for copy in copies[1:4]:
        copy.wait()
    streams, frames, kv_width = k_buf.shape
    heads = q_ref.shape[1] // HEAD_DIM
    group = heads // (kv_width // HEAD_DIM)
    scale = 1.0 / math.sqrt(HEAD_DIM)
    query = q_ref[...].astype(F32)
    new_key = nk_ref[...].astype(F32)
    zero = jnp.zeros((streams, HEAD_DIM), F32)
    rows, new_scores = [], []
    for h in range(heads):
        g = h // group
        q = query[:, h * HEAD_DIM : (h + 1) * HEAD_DIM]
        rows.append(
            jnp.concatenate([q if b == g else zero for b in range(kv_width // HEAD_DIM)], axis=1)
        )
        k = new_key[:, g * HEAD_DIM : (g + 1) * HEAD_DIM]
        new_scores.append(jnp.sum(q * k, axis=1, keepdims=True) * scale)
    spread = jnp.concatenate(rows, axis=0).astype(BF16)
    row = lax.broadcasted_iota(jnp.int32, (streams, streams * frames), 0)
    col = lax.broadcasted_iota(jnp.int32, (streams, streams * frames), 1)
    end = jnp.zeros_like(row)
    for s in range(streams):
        end = jnp.where(row == s, len_ref[s] + s * frames, end)
    valid = (col >= row * frames) & (col < end)
    copies[0].wait()
    scores = lax.dot_general(
        spread,
        k_buf[...].reshape(streams * frames, kv_width),
        (((1,), (1,)), ((), ())),
        preferred_element_type=F32,
    )
    probs, new_probs = [], []
    for h in range(heads):
        old = jnp.where(valid, scores[h * streams : (h + 1) * streams] * scale, -1e30)
        new = new_scores[h]
        top = jnp.maximum(jnp.max(old, axis=1, keepdims=True), new)
        old = jnp.exp(old - top)
        new = jnp.exp(new - top)
        total = jnp.sum(old, axis=1, keepdims=True) + new
        probs.append(old / total)
        new_probs.append((new / total).astype(BF16).astype(F32))
    probs = jnp.concatenate(probs, axis=0).astype(BF16)
    copies[4].wait()
    copies[5].wait()
    context = jnp.dot(
        probs, v_buf[...].reshape(streams * frames, kv_width), preferred_element_type=F32
    )
    new_value = nv_ref[...].astype(F32)
    width = ctx_ref.shape[2]
    for h in range(heads):
        c = (h // group) * HEAD_DIM
        part = context[h * streams : (h + 1) * streams, c : c + HEAD_DIM]
        part = part + new_probs[h] * new_value[:, c : c + HEAD_DIM]
        at = h * HEAD_DIM
        ctx_ref[at // width, :, at % width : at % width + HEAD_DIM] = part
    me = lax.axis_index("sub")
    for step, out_ref in zip(steps, out_refs):
        out_ref[...] = ctx_ref[jnp.bitwise_xor(me, step)].astype(BF16)
    for copy in copies[6:]:
        copy.wait()
    gates = gates_ref[...]
    weights = gates / jnp.sum(gates, axis=1, keepdims=True)
    ids = ids_ref[...]
    lane = lax.broadcasted_iota(jnp.int32, table_ref.shape, 1)
    label = jnp.where(lane >= experts, lane - experts, lane)
    table = jnp.zeros(lane.shape, F32)
    for k in range(ids.shape[1]):
        table = table + jnp.where(label == ids[:, k : k + 1], weights[:, k : k + 1], 0.0)
    high = table.astype(BF16).astype(F32)
    table_ref[...] = jnp.where(lane < experts, high, table - high).astype(BF16)


def project_kernel(count, *refs):
    x = jnp.concatenate([ref[...].astype(F32) for ref in refs[:count]], axis=0).astype(BF16)
    y = jnp.dot(x, refs[count][...], preferred_element_type=F32)
    streams = refs[0].shape[0]
    for i, ref in enumerate(refs[-count:]):
        ref[...] = y[i * streams : (i + 1) * streams].astype(ref.dtype)


def norm_kernel(count, *refs):
    res_ref, gain_ref, table_ref, _, _, hidden_ref, out_ref = refs[count:]
    hidden = res_ref[...].astype(F32)
    for ref in refs[:count]:
        hidden = hidden + ref[...].astype(F32)
    hidden_ref[...] = hidden
    width = hidden.shape[1]
    normed = hidden * lax.rsqrt(jnp.mean(hidden * hidden, axis=1, keepdims=True) + 1e-06)
    normed = (normed * gain_ref[...].astype(F32).reshape(1, width)).astype(BF16)
    out_ref[:, :width] = normed
    out_ref[:, width:] = table_ref[...]


def join_kernel(*refs):
    refs[-1][...] = jnp.concatenate([ref[...].astype(F32) for ref in refs[:-1]], axis=0).astype(BF16)


def expert_kernel(experts, count, *refs):
    full = jnp.concatenate([ref[...].astype(F32) for ref in refs[:count]], axis=0)
    weight_refs, out_refs = refs[count : count + 6], refs[count + 6 :]
    step, width = out_refs[0].shape
    rows = full[:, :width].astype(BF16)
    table = full[:, width:]
    lane = lax.broadcasted_iota(jnp.int32, table.shape, 1)
    major, minor, n_sub = lax.axis_index("expert"), lax.axis_index("sub"), lax.axis_size("sub")
    total = None
    for i, place in enumerate((major, jnp.bitwise_xor(major, 1))):
        gate_ref, up_ref, down_ref = weight_refs[3 * i : 3 * i + 3]
        expert = place * n_sub + minor
        chosen = (lane == expert) | (lane == expert + experts)
        weight = jnp.sum(jnp.where(chosen, table, 0.0), axis=1, keepdims=True)
        gate = jnp.dot(rows, gate_ref[...], preferred_element_type=F32)
        up = jnp.dot(rows, up_ref[...], preferred_element_type=F32)
        act = (gate / (1.0 + jnp.exp(-gate)) * up).astype(BF16)
        y = jnp.dot(act, down_ref[...], preferred_element_type=F32) * weight
        total = y if total is None else total + y
    for i, ref in enumerate(out_refs):
        ref[...] = total[i * step : (i + 1) * step].astype(ref.dtype)


def fold_kernel(count, *refs):
    total = refs[0][...]
    for ref in refs[1:count]:
        total = total + ref[...].astype(F32)
    step = refs[count].shape[0]
    for i, ref in enumerate(refs[count:]):
        ref[...] = total[i * step : (i + 1) * step].astype(ref.dtype)


def finish_kernel(*refs):
    total = refs[0][...]
    for ref in refs[1:-1]:
        total = total + ref[...].astype(F32)
    refs[-1][...] = total.astype(BF16)


def body(
    residual,
    query,
    new_key,
    new_value,
    key_cache,
    value_cache,
    cache_len,
    out_weight,
    norm_gain,
    expert_ids,
    gate_scores,
    expert_gate,
    expert_up,
    expert_down,
):
    streams, width = residual.shape
    n_expert, n_sub = lax.axis_size("expert"), lax.axis_size("sub")
    experts = n_expert * n_sub
    twins = [(i, i ^ 1) for i in range(n_expert)]
    shape = jax.ShapeDtypeStruct

    table_width = -(-2 * experts // LANES) * LANES
    mine = (expert_gate, expert_up, expert_down)
    twin = [lax.ppermute(w, "expert", twins) for w in mine[:2]]

    steps = (0, *range(n_sub - 1, 0, -1))
    chip_steps = (0, *range(n_expert - 2, 0, -2))

    def exchange(blocks, axis="sub"):
        size, order = (n_sub, steps) if axis == "sub" else (n_expert, chip_steps)
        sent = [
            lax.ppermute(block, axis, [(i, i ^ step) for i in range(size)])
            for step, block in zip(order[1:], blocks[1:])
        ]
        return [blocks[0], *sent]

    def gather(block):
        sent = [
            lax.ppermute(block, "sub", [(i, i ^ step) for i in range(n_sub)])
            for step in reversed(steps[1:])
        ]
        return [block, *reversed(sent)]

    *context, resident, table, out_weight, norm_gain = pl.pallas_call(
        functools.partial(attend_kernel, experts, steps),
        out_shape=(
            *(shape((streams, width // n_sub), BF16) for _ in steps),
            shape(residual.shape, BF16),
            shape((streams, table_width), BF16),
            pltpu.VMEM(out_weight.shape, BF16),
            pltpu.VMEM(norm_gain.shape, BF16),
        ),
        in_specs=[HBM] * 11,
        out_specs=(VMEM,) * (n_sub + 4),
        scratch_shapes=[
            pltpu.VMEM((n_sub, streams, width // n_sub), F32),
            pltpu.SMEM(cache_len.shape, jnp.int32),
            pltpu.VMEM(query.shape, BF16),
            pltpu.VMEM(new_key.shape, BF16),
            pltpu.VMEM(new_value.shape, BF16),
            pltpu.VMEM(key_cache.shape, BF16),
            pltpu.VMEM(value_cache.shape, BF16),
            pltpu.VMEM(expert_ids.shape, jnp.int32),
            pltpu.VMEM(gate_scores.shape, F32),
            pltpu.SemaphoreType.DMA((11,)),
        ],
        compiler_params=params(12),
        name="attend",
    )(
        *(
            in_hbm(a)
            for a in (
                cache_len,
                query,
                new_key,
                new_value,
                key_cache,
                value_cache,
                residual,
                expert_ids,
                gate_scores,
                out_weight,
                norm_gain,
            )
        )
    )
    context, last, twin[0] = lax.optimization_barrier((exchange(context), expert_down, twin[0]))
    twin.append(lax.ppermute(last, "expert", twins))
    partial = pl.pallas_call(
        functools.partial(project_kernel, n_sub),
        out_shape=tuple(shape((streams, width), BF16 if step else F32) for step in steps),
        in_specs=[VMEM] * (n_sub + 1) + [HBM],
        out_specs=(VMEM,) * n_sub,
        compiler_params=params(8),
        name="project",
    )(*context, out_weight, in_hbm(expert_gate[0]))

    hidden, rows = pl.pallas_call(
        functools.partial(norm_kernel, n_sub),
        out_shape=(
            shape((streams, width), F32),
            shape((streams, width + table_width), BF16),
        ),
        in_specs=[VMEM] * (n_sub + 3) + [HBM] * 2,
        out_specs=(VMEM, VMEM),
        compiler_params=params(8),
        name="norm",
    )(
        *exchange(partial),
        resident,
        norm_gain,
        table,
        in_hbm(expert_up[0]),
        in_hbm(expert_down[0]),
    )
    chips = len(chip_steps)
    rows = pl.pallas_call(
        join_kernel,
        out_shape=shape((chips * streams, width + table_width), BF16),
        in_specs=[VMEM] * chips,
        out_specs=VMEM,
        compiler_params=params(4),
        name="join",
    )(*exchange([rows] * chips, "expert"))
    summed = pl.pallas_call(
        functools.partial(expert_kernel, experts, n_sub),
        out_shape=tuple(shape((chips * streams, width), BF16 if step else F32) for step in steps),
        in_specs=[VMEM] * (n_sub + 6),
        out_specs=(VMEM,) * n_sub,
        compiler_params=params(8 + experts * streams // 64),
        name="expert",
    )(*gather(rows), *(in_vmem(w[0]) for w in (*mine, *twin)))
    summed = pl.pallas_call(
        functools.partial(fold_kernel, n_sub),
        out_shape=tuple(shape((streams, width), BF16 if step else F32) for step in chip_steps),
        in_specs=[VMEM] * n_sub,
        out_specs=(VMEM,) * chips,
        compiler_params=params(8),
        name="fold",
    )(*exchange(summed))
    return pl.pallas_call(
        finish_kernel,
        out_shape=shape((streams, width), BF16),
        in_specs=[VMEM] * (chips + 1),
        out_specs=VMEM,
        compiler_params=params(4),
        name="finish",
    )(hidden, *exchange(summed, "expert"))


def solution(mesh):
    rows = P(("groups", "expert", "sub"), None)
    cache = P(("groups", "expert", "sub"), None, None)
    weights = P(("expert", "sub"), None, None)
    return jax.shard_map(
        body,
        mesh=mesh,
        in_specs=(
            rows,
            rows,
            rows,
            rows,
            cache,
            cache,
            P(("groups", "expert", "sub")),
            P("sub", None),
            P(),
            rows,
            rows,
            weights,
            weights,
            weights,
        ),
        out_specs=rows,
        check_vma=False,
    )
```

```python
import functools
import math

import jax
import jax.numpy as jnp
from jax import lax
from jax.experimental import pallas as pl
from jax.experimental.pallas import tpu as pltpu
from jax.sharding import PartitionSpec as P

HEAD_DIM = 128
LANES = 128
BF16, F32 = jnp.bfloat16, jnp.float32
VMEM = pl.BlockSpec(memory_space=pltpu.VMEM)
SMEM = pl.BlockSpec(memory_space=pltpu.SMEM)
HBM = pl.BlockSpec(memory_space=pltpu.HBM)
def params(mib):
    return pltpu.CompilerParams(vmem_limit_bytes=mib * 2**20)


def in_hbm(x):
    return pltpu.with_memory_space_constraint(x, pltpu.HBM)


def in_vmem(x):
    return pltpu.with_memory_space_constraint(x, pltpu.VMEM)


def attend_kernel(
    experts,
    len_hbm,
    q_hbm,
    nk_hbm,
    nv_hbm,
    k_hbm,
    v_hbm,
    res_hbm,
    ids_hbm,
    gates_hbm,
    gain_hbm,
    *refs,
):
    (
        ctx_ref,
        res_ref,
        table_ref,
        gain_ref,
        len_ref,
        q_ref,
        nk_ref,
        nv_ref,
        k_buf,
        v_buf,
        ids_ref,
        gates_ref,
        sems,
    ) = refs
    pairs = (
        (k_hbm, k_buf),
        (q_hbm, q_ref),
        (nk_hbm, nk_ref),
        (len_hbm, len_ref),
        (v_hbm, v_buf),
        (nv_hbm, nv_ref),
        (ids_hbm, ids_ref),
        (gates_hbm, gates_ref),
        (res_hbm, res_ref),
        (gain_hbm, gain_ref),
    )
    copies = [pltpu.make_async_copy(a, b, sems.at[i]) for i, (a, b) in enumerate(pairs)]
    for copy in copies:
        copy.start()
    for copy in copies[1:4]:
        copy.wait()
    streams, frames, kv_width = k_buf.shape
    heads = q_ref.shape[1] // HEAD_DIM
    group = heads // (kv_width // HEAD_DIM)
    scale = 1.0 / math.sqrt(HEAD_DIM)
    query = q_ref[...].astype(F32)
    new_key = nk_ref[...].astype(F32)
    zero = jnp.zeros((streams, HEAD_DIM), F32)
    rows, new_scores = [], []
    for h in range(heads):
        g = h // group
        q = query[:, h * HEAD_DIM : (h + 1) * HEAD_DIM]
        rows.append(
            jnp.concatenate([q if b == g else zero for b in range(kv_width // HEAD_DIM)], axis=1)
        )
        k = new_key[:, g * HEAD_DIM : (g + 1) * HEAD_DIM]
        new_scores.append(jnp.sum(q * k, axis=1, keepdims=True) * scale)
    spread = jnp.concatenate(rows, axis=0).astype(BF16)
    row = lax.broadcasted_iota(jnp.int32, (streams, frames), 0)
    col = lax.broadcasted_iota(jnp.int32, (streams, frames), 1)
    held = jnp.zeros_like(row)
    for s in range(streams):
        held = jnp.where(row == s, len_ref[s], held)
    copies[0].wait()
    scores = lax.dot_general(
        spread,
        k_buf[...].reshape(streams * frames, kv_width),
        (((1,), (1,)), ((), ())),
        preferred_element_type=F32,
    )
    probs, new_probs = [], []
    for h in range(heads):
        block = scores[h * streams : (h + 1) * streams]
        old = block[:, :frames]
        for s in range(1, streams):
            old = jnp.where(row == s, block[:, s * frames : (s + 1) * frames], old)
        old = jnp.where(col < held, old * scale, -1e30)
        new = new_scores[h]
        top = jnp.maximum(jnp.max(old, axis=1, keepdims=True), new)
        old = jnp.exp(old - top)
        new = jnp.exp(new - top)
        total = jnp.sum(old, axis=1, keepdims=True) + new
        old = old / total
        probs.append(
            jnp.concatenate([jnp.where(row == s, old, 0.0) for s in range(streams)], axis=1)
        )
        new_probs.append((new / total).astype(BF16).astype(F32))
    probs = jnp.concatenate(probs, axis=0).astype(BF16)
    copies[4].wait()
    copies[5].wait()
    context = jnp.dot(
        probs, v_buf[...].reshape(streams * frames, kv_width), preferred_element_type=F32
    )
    new_value = nv_ref[...].astype(F32)
    width = ctx_ref.shape[2]
    for h in range(heads):
        c = (h // group) * HEAD_DIM
        part = context[h * streams : (h + 1) * streams, c : c + HEAD_DIM]
        part = part + new_probs[h] * new_value[:, c : c + HEAD_DIM]
        at = h * HEAD_DIM
        ctx_ref[at // width, :, at % width : at % width + HEAD_DIM] = part
    for copy in copies[6:]:
        copy.wait()
    gates = gates_ref[...]
    weights = gates / jnp.sum(gates, axis=1, keepdims=True)
    ids = ids_ref[...]
    lane = lax.broadcasted_iota(jnp.int32, table_ref.shape, 1)
    label = jnp.where(lane >= experts, lane - experts, lane)
    table = jnp.zeros(lane.shape, F32)
    for k in range(ids.shape[1]):
        table = table + jnp.where(label == ids[:, k : k + 1], weights[:, k : k + 1], 0.0)
    high = table.astype(BF16).astype(F32)
    table_ref[...] = jnp.where(lane < experts, high, table - high).astype(BF16)


def route_kernel(steps, ctx_ref, _, *refs):
    me = lax.axis_index("sub")
    for step, ref in zip(steps, refs):
        ref[...] = ctx_ref[jnp.bitwise_xor(me, step)].astype(BF16)


def project_kernel(count, *refs):
    x = jnp.concatenate([ref[...].astype(F32) for ref in refs[:count]], axis=0).astype(BF16)
    y = jnp.dot(x, refs[count][...], preferred_element_type=F32)
    streams = refs[0].shape[0]
    for i, ref in enumerate(refs[-count:]):
        ref[...] = y[i * streams : (i + 1) * streams].astype(ref.dtype)


def norm_kernel(count, *refs):
    res_ref, gain_ref, table_ref, _, _, hidden_ref, out_ref = refs[count:]
    hidden = res_ref[...].astype(F32)
    for ref in refs[:count]:
        hidden = hidden + ref[...].astype(F32)
    hidden_ref[...] = hidden
    width = hidden.shape[1]
    normed = hidden * lax.rsqrt(jnp.mean(hidden * hidden, axis=1, keepdims=True) + 1e-06)
    normed = (normed * gain_ref[...].astype(F32).reshape(1, width)).astype(BF16)
    out_ref[:, :width] = normed
    out_ref[:, width:] = table_ref[...]


def join_kernel(*refs):
    refs[-1][...] = jnp.concatenate([ref[...].astype(F32) for ref in refs[:-1]], axis=0).astype(BF16)


def expert_kernel(experts, count, *refs):
    full = jnp.concatenate([ref[...].astype(F32) for ref in refs[:count]], axis=0)
    weight_refs, out_refs = refs[count : count + 6], refs[count + 6 :]
    step, width = out_refs[0].shape
    spare = 128 - full.shape[0]
    if spare > 0:
        full = jnp.concatenate([full, jnp.zeros((spare, full.shape[1]), F32)], axis=0)
    rows = full[:, :width].astype(BF16)
    table = full[:, width:]
    lane = lax.broadcasted_iota(jnp.int32, table.shape, 1)
    major, minor, n_sub = lax.axis_index("expert"), lax.axis_index("sub"), lax.axis_size("sub")
    total = None
    for i, place in enumerate((major, jnp.bitwise_xor(major, 1))):
        gate_ref, up_ref, down_ref = weight_refs[3 * i : 3 * i + 3]
        expert = place * n_sub + minor
        chosen = (lane == expert) | (lane == expert + experts)
        weight = jnp.sum(jnp.where(chosen, table, 0.0), axis=1, keepdims=True)
        gate = jnp.dot(rows, gate_ref[...], preferred_element_type=F32)
        up = jnp.dot(rows, up_ref[...], preferred_element_type=F32)
        act = (gate / (1.0 + jnp.exp(-gate)) * up).astype(BF16)
        y = jnp.dot(act, down_ref[...], preferred_element_type=F32) * weight
        total = y if total is None else total + y
    for i, ref in enumerate(out_refs):
        ref[...] = total[i * step : (i + 1) * step].astype(ref.dtype)


def fold_kernel(count, *refs):
    total = refs[0][...]
    for ref in refs[1:count]:
        total = total + ref[...].astype(F32)
    step = refs[count].shape[0]
    for i, ref in enumerate(refs[count:]):
        ref[...] = total[i * step : (i + 1) * step].astype(ref.dtype)


def finish_kernel(*refs):
    total = refs[0][...]
    for ref in refs[1:-1]:
        total = total + ref[...].astype(F32)
    refs[-1][...] = total.astype(BF16)


def body(
    residual,
    query,
    new_key,
    new_value,
    key_cache,
    value_cache,
    cache_len,
    out_weight,
    norm_gain,
    expert_ids,
    gate_scores,
    expert_gate,
    expert_up,
    expert_down,
):
    streams, width = residual.shape
    n_expert, n_sub = lax.axis_size("expert"), lax.axis_size("sub")
    experts = n_expert * n_sub
    twins = [(i, i ^ 1) for i in range(n_expert)]
    shape = jax.ShapeDtypeStruct

    table_width = -(-2 * experts // LANES) * LANES
    mine = (expert_gate, expert_up, expert_down)
    twin = [lax.ppermute(w, "expert", twins) for w in mine[:2]]

    steps = (0, *range(n_sub - 1, 0, -1))
    chip_steps = (0, *range(n_expert - 2, 0, -2))

    def exchange(blocks, axis="sub"):
        size, order = (n_sub, steps) if axis == "sub" else (n_expert, chip_steps)
        sent = [
            lax.ppermute(block, axis, [(i, i ^ step) for i in range(size)])
            for step, block in zip(order[1:], blocks[1:])
        ]
        return [blocks[0], *sent]

    def gather(block):
        sent = [
            lax.ppermute(block, "sub", [(i, i ^ step) for i in range(n_sub)])
            for step in reversed(steps[1:])
        ]
        return [block, *reversed(sent)]

    context, resident, table, norm_gain = pl.pallas_call(
        functools.partial(attend_kernel, experts),
        out_shape=(
            shape((n_sub, streams, width // n_sub), F32),
            shape(residual.shape, BF16),
            shape((streams, table_width), BF16),
            pltpu.VMEM(norm_gain.shape, BF16),
        ),
        in_specs=[HBM] * 10,
        out_specs=(VMEM,) * 4,
        scratch_shapes=[
            pltpu.SMEM(cache_len.shape, jnp.int32),
            pltpu.VMEM(query.shape, BF16),
            pltpu.VMEM(new_key.shape, BF16),
            pltpu.VMEM(new_value.shape, BF16),
            pltpu.VMEM(key_cache.shape, BF16),
            pltpu.VMEM(value_cache.shape, BF16),
            pltpu.VMEM(expert_ids.shape, jnp.int32),
            pltpu.VMEM(gate_scores.shape, F32),
            pltpu.SemaphoreType.DMA((10,)),
        ],
        compiler_params=params(12),
        name="attend",
    )(
        *(
            in_hbm(a)
            for a in (
                cache_len,
                query,
                new_key,
                new_value,
                key_cache,
                value_cache,
                residual,
                expert_ids,
                gate_scores,
                norm_gain,
            )
        )
    )
    context = pl.pallas_call(
        functools.partial(route_kernel, steps),
        out_shape=(shape((streams, width // n_sub), BF16),) * n_sub,
        in_specs=[VMEM, HBM],
        out_specs=(VMEM,) * n_sub,
        compiler_params=params(4),
        name="route",
    )(context, in_hbm(expert_gate[0]))
    context, last, twin[0] = lax.optimization_barrier((exchange(context), expert_down, twin[0]))
    twin.append(lax.ppermute(last, "expert", twins))
    partial = pl.pallas_call(
        functools.partial(project_kernel, n_sub),
        out_shape=tuple(shape((streams, width), BF16 if step else F32) for step in steps),
        in_specs=[VMEM] * (n_sub + 1) + [HBM],
        out_specs=(VMEM,) * n_sub,
        compiler_params=params(8),
        name="project",
    )(*context, in_vmem(out_weight), in_hbm(expert_gate[0]))

    hidden, rows = pl.pallas_call(
        functools.partial(norm_kernel, n_sub),
        out_shape=(
            shape((streams, width), F32),
            shape((streams, width + table_width), BF16),
        ),
        in_specs=[VMEM] * (n_sub + 3) + [HBM] * 2,
        out_specs=(VMEM, VMEM),
        compiler_params=params(8),
        name="norm",
    )(
        *exchange(partial),
        resident,
        norm_gain,
        table,
        in_hbm(expert_up[0]),
        in_hbm(expert_down[0]),
    )
    chips = len(chip_steps)
    rows = pl.pallas_call(
        join_kernel,
        out_shape=shape((chips * streams, width + table_width), BF16),
        in_specs=[VMEM] * chips,
        out_specs=VMEM,
        compiler_params=params(4),
        name="join",
    )(*exchange([rows] * chips, "expert"))
    summed = pl.pallas_call(
        functools.partial(expert_kernel, experts, n_sub),
        out_shape=tuple(shape((chips * streams, width), BF16 if step else F32) for step in steps),
        in_specs=[VMEM] * (n_sub + 6),
        out_specs=(VMEM,) * n_sub,
        compiler_params=params(8 + experts * streams // 64),
        name="expert",
    )(*gather(rows), *(in_vmem(w[0]) for w in (*mine, *twin)))
    summed = pl.pallas_call(
        functools.partial(fold_kernel, n_sub),
        out_shape=tuple(shape((streams, width), BF16 if step else F32) for step in chip_steps),
        in_specs=[VMEM] * n_sub,
        out_specs=(VMEM,) * chips,
        compiler_params=params(8),
        name="fold",
    )(*exchange(summed))
    return pl.pallas_call(
        finish_kernel,
        out_shape=shape((streams, width), BF16),
        in_specs=[VMEM] * (chips + 1),
        out_specs=VMEM,
        compiler_params=params(4),
        name="finish",
    )(hidden, *exchange(summed, "expert"))


def solution(mesh):
    rows = P(("groups", "expert", "sub"), None)
    cache = P(("groups", "expert", "sub"), None, None)
    weights = P(("expert", "sub"), None, None)
    return jax.shard_map(
        body,
        mesh=mesh,
        in_specs=(
            rows,
            rows,
            rows,
            rows,
            cache,
            cache,
            P(("groups", "expert", "sub")),
            P("sub", None),
            P(),
            rows,
            rows,
            weights,
            weights,
            weights,
        ),
        out_specs=rows,
        check_vma=False,
    )
```

```python
import functools
import math

import jax
import jax.numpy as jnp
from jax import lax
from jax.experimental import pallas as pl
from jax.experimental.pallas import tpu as pltpu
from jax.sharding import PartitionSpec as P

HEAD_DIM = 128
LANES = 128
BF16, F32 = jnp.bfloat16, jnp.float32
VMEM = pl.BlockSpec(memory_space=pltpu.VMEM)
SMEM = pl.BlockSpec(memory_space=pltpu.SMEM)
HBM = pl.BlockSpec(memory_space=pltpu.HBM)
def params(mib):
    return pltpu.CompilerParams(vmem_limit_bytes=mib * 2**20)


def in_hbm(x):
    return pltpu.with_memory_space_constraint(x, pltpu.HBM)


def in_vmem(x):
    return pltpu.with_memory_space_constraint(x, pltpu.VMEM)


def attend_kernel(
    experts,
    len_hbm,
    q_hbm,
    nk_hbm,
    nv_hbm,
    k_hbm,
    v_hbm,
    res_hbm,
    ids_hbm,
    gates_hbm,
    gain_hbm,
    *refs,
):
    (
        ctx_ref,
        res_ref,
        table_ref,
        gain_ref,
        len_ref,
        q_ref,
        nk_ref,
        nv_ref,
        k_buf,
        v_buf,
        ids_ref,
        gates_ref,
        sems,
    ) = refs
    pairs = (
        (k_hbm, k_buf),
        (q_hbm, q_ref),
        (nk_hbm, nk_ref),
        (len_hbm, len_ref),
        (v_hbm, v_buf),
        (nv_hbm, nv_ref),
        (ids_hbm, ids_ref),
        (gates_hbm, gates_ref),
        (res_hbm, res_ref),
        (gain_hbm, gain_ref),
    )
    copies = [pltpu.make_async_copy(a, b, sems.at[i]) for i, (a, b) in enumerate(pairs)]
    for copy in copies:
        copy.start()
    for copy in copies[1:4]:
        copy.wait()
    streams, frames, kv_width = k_buf.shape
    heads = q_ref.shape[1] // HEAD_DIM
    group = heads // (kv_width // HEAD_DIM)
    scale = 1.0 / math.sqrt(HEAD_DIM)
    query = q_ref[...].astype(F32)
    new_key = nk_ref[...].astype(F32)
    zero = jnp.zeros((streams, HEAD_DIM), F32)
    rows, new_scores = [], []
    for h in range(heads):
        g = h // group
        q = query[:, h * HEAD_DIM : (h + 1) * HEAD_DIM]
        rows.append(
            jnp.concatenate([q if b == g else zero for b in range(kv_width // HEAD_DIM)], axis=1)
        )
        k = new_key[:, g * HEAD_DIM : (g + 1) * HEAD_DIM]
        new_scores.append(jnp.sum(q * k, axis=1, keepdims=True) * scale)
    spread = jnp.concatenate(rows, axis=0).astype(BF16)
    row = lax.broadcasted_iota(jnp.int32, (streams, frames), 0)
    col = lax.broadcasted_iota(jnp.int32, (streams, frames), 1)
    held = jnp.zeros_like(row)
    for s in range(streams):
        held = jnp.where(row == s, len_ref[s], held)
    copies[0].wait()
    scores = lax.dot_general(
        spread,
        k_buf[...].reshape(streams * frames, kv_width),
        (((1,), (1,)), ((), ())),
        preferred_element_type=F32,
    )
    probs, new_probs = [], []
    for h in range(heads):
        block = scores[h * streams : (h + 1) * streams]
        old = block[:, :frames]
        for s in range(1, streams):
            old = jnp.where(row == s, block[:, s * frames : (s + 1) * frames], old)
        old = jnp.where(col < held, old * scale, -1e30)
        new = new_scores[h]
        top = jnp.maximum(jnp.max(old, axis=1, keepdims=True), new)
        old = jnp.exp(old - top)
        new = jnp.exp(new - top)
        total = jnp.sum(old, axis=1, keepdims=True) + new
        old = old / total
        probs.append(
            jnp.concatenate([jnp.where(row == s, old, 0.0) for s in range(streams)], axis=1)
        )
        new_probs.append((new / total).astype(BF16).astype(F32))
    probs = jnp.concatenate(probs, axis=0).astype(BF16)
    copies[4].wait()
    copies[5].wait()
    context = jnp.dot(
        probs, v_buf[...].reshape(streams * frames, kv_width), preferred_element_type=F32
    )
    new_value = nv_ref[...].astype(F32)
    width = ctx_ref.shape[2]
    for h in range(heads):
        c = (h // group) * HEAD_DIM
        part = context[h * streams : (h + 1) * streams, c : c + HEAD_DIM]
        part = part + new_probs[h] * new_value[:, c : c + HEAD_DIM]
        at = h * HEAD_DIM
        ctx_ref[at // width, :, at % width : at % width + HEAD_DIM] = part
    for copy in copies[6:]:
        copy.wait()
    gates = gates_ref[...]
    weights = gates / jnp.sum(gates, axis=1, keepdims=True)
    ids = ids_ref[...]
    lane = lax.broadcasted_iota(jnp.int32, table_ref.shape, 1)
    label = jnp.where(lane >= experts, lane - experts, lane)
    table = jnp.zeros(lane.shape, F32)
    for k in range(ids.shape[1]):
        table = table + jnp.where(label == ids[:, k : k + 1], weights[:, k : k + 1], 0.0)
    high = table.astype(BF16).astype(F32)
    table_ref[...] = jnp.where(lane < experts, high, table - high).astype(BF16)


def route_kernel(steps, ctx_ref, _, *refs):
    me = lax.axis_index("sub")
    for step, ref in zip(steps, refs):
        ref[...] = ctx_ref[jnp.bitwise_xor(me, step)].astype(BF16)


def project_kernel(count, *refs):
    x = jnp.concatenate([ref[...].astype(F32) for ref in refs[:count]], axis=0).astype(BF16)
    y = jnp.dot(x, refs[count][...], preferred_element_type=F32)
    streams = refs[0].shape[0]
    for i, ref in enumerate(refs[-count:]):
        ref[...] = y[i * streams : (i + 1) * streams].astype(ref.dtype)


def norm_kernel(count, *refs):
    res_ref, gain_ref, table_ref, _, _, hidden_ref, out_ref = refs[count:]
    hidden = res_ref[...].astype(F32)
    for ref in refs[:count]:
        hidden = hidden + ref[...].astype(F32)
    hidden_ref[...] = hidden
    width = hidden.shape[1]
    normed = hidden * lax.rsqrt(jnp.mean(hidden * hidden, axis=1, keepdims=True) + 1e-06)
    normed = (normed * gain_ref[...].astype(F32).reshape(1, width)).astype(BF16)
    out_ref[:, :width] = normed
    out_ref[:, width:] = table_ref[...]


def join_kernel(*refs):
    refs[-1][...] = jnp.concatenate([ref[...].astype(F32) for ref in refs[:-1]], axis=0).astype(BF16)


def expert_kernel(experts, count, *refs):
    full = jnp.concatenate([ref[...].astype(F32) for ref in refs[:count]], axis=0)
    weight_refs, out_refs = refs[count : count + 6], refs[count + 6 :]
    step, width = out_refs[0].shape
    spare = 128 - full.shape[0]
    if spare > 0:
        full = jnp.concatenate([full, jnp.zeros((spare, full.shape[1]), F32)], axis=0)
    rows = full[:, :width].astype(BF16)
    table = full[:, width:]
    lane = lax.broadcasted_iota(jnp.int32, table.shape, 1)
    major, minor, n_sub = lax.axis_index("expert"), lax.axis_index("sub"), lax.axis_size("sub")
    acts, weights = [], []
    for i, place in enumerate((major, jnp.bitwise_xor(major, 1))):
        expert = place * n_sub + minor
        chosen = (lane == expert) | (lane == expert + experts)
        weights.append(jnp.sum(jnp.where(chosen, table, 0.0), axis=1, keepdims=True))
        gate = jnp.dot(rows, weight_refs[3 * i][...], preferred_element_type=F32)
        up = jnp.dot(rows, weight_refs[3 * i + 1][...], preferred_element_type=F32)
        acts.append((gate / (1.0 + jnp.exp(-gate)) * up).astype(BF16))
    total = weights[0] * jnp.dot(acts[0], weight_refs[2][...], preferred_element_type=F32)
    total = total + weights[1] * jnp.dot(acts[1], weight_refs[5][...], preferred_element_type=F32)
    for i, ref in enumerate(out_refs):
        ref[...] = total[i * step : (i + 1) * step].astype(ref.dtype)


def fold_kernel(count, *refs):
    total = refs[0][...]
    for ref in refs[1:count]:
        total = total + ref[...].astype(F32)
    step = refs[count].shape[0]
    for i, ref in enumerate(refs[count:]):
        ref[...] = total[i * step : (i + 1) * step].astype(ref.dtype)


def finish_kernel(*refs):
    total = refs[0][...]
    for ref in refs[1:-1]:
        total = total + ref[...].astype(F32)
    refs[-1][...] = total.astype(BF16)


def body(
    residual,
    query,
    new_key,
    new_value,
    key_cache,
    value_cache,
    cache_len,
    out_weight,
    norm_gain,
    expert_ids,
    gate_scores,
    expert_gate,
    expert_up,
    expert_down,
):
    streams, width = residual.shape
    n_expert, n_sub = lax.axis_size("expert"), lax.axis_size("sub")
    experts = n_expert * n_sub
    twins = [(i, i ^ 1) for i in range(n_expert)]
    shape = jax.ShapeDtypeStruct

    table_width = -(-2 * experts // LANES) * LANES
    mine = (expert_gate, expert_up, expert_down)
    twin = [lax.ppermute(w, "expert", twins) for w in mine[:2]]

    steps = (0, *range(n_sub - 1, 0, -1))
    chip_steps = (0, *range(n_expert - 2, 0, -2))

    def exchange(blocks, axis="sub"):
        size, order = (n_sub, steps) if axis == "sub" else (n_expert, chip_steps)
        sent = [
            lax.ppermute(block, axis, [(i, i ^ step) for i in range(size)])
            for step, block in zip(order[1:], blocks[1:])
        ]
        return [blocks[0], *sent]

    def gather(block):
        sent = [
            lax.ppermute(block, "sub", [(i, i ^ step) for i in range(n_sub)])
            for step in reversed(steps[1:])
        ]
        return [block, *reversed(sent)]

    context, resident, table, norm_gain = pl.pallas_call(
        functools.partial(attend_kernel, experts),
        out_shape=(
            shape((n_sub, streams, width // n_sub), F32),
            shape(residual.shape, BF16),
            shape((streams, table_width), BF16),
            pltpu.VMEM(norm_gain.shape, BF16),
        ),
        in_specs=[HBM] * 10,
        out_specs=(VMEM,) * 4,
        scratch_shapes=[
            pltpu.SMEM(cache_len.shape, jnp.int32),
            pltpu.VMEM(query.shape, BF16),
            pltpu.VMEM(new_key.shape, BF16),
            pltpu.VMEM(new_value.shape, BF16),
            pltpu.VMEM(key_cache.shape, BF16),
            pltpu.VMEM(value_cache.shape, BF16),
            pltpu.VMEM(expert_ids.shape, jnp.int32),
            pltpu.VMEM(gate_scores.shape, F32),
            pltpu.SemaphoreType.DMA((10,)),
        ],
        compiler_params=params(12),
        name="attend",
    )(
        *(
            in_hbm(a)
            for a in (
                cache_len,
                query,
                new_key,
                new_value,
                key_cache,
                value_cache,
                residual,
                expert_ids,
                gate_scores,
                norm_gain,
            )
        )
    )
    context = pl.pallas_call(
        functools.partial(route_kernel, steps),
        out_shape=(shape((streams, width // n_sub), BF16),) * n_sub,
        in_specs=[VMEM, HBM],
        out_specs=(VMEM,) * n_sub,
        compiler_params=params(4),
        name="route",
    )(context, in_hbm(expert_gate[0]))
    context, last, twin[0] = lax.optimization_barrier((exchange(context), expert_down, twin[0]))
    twin.append(lax.ppermute(last, "expert", twins))
    partial = pl.pallas_call(
        functools.partial(project_kernel, n_sub),
        out_shape=tuple(shape((streams, width), BF16 if step else F32) for step in steps),
        in_specs=[VMEM] * (n_sub + 1) + [HBM],
        out_specs=(VMEM,) * n_sub,
        compiler_params=params(8),
        name="project",
    )(*context, in_vmem(out_weight), in_hbm(expert_gate[0]))

    hidden, rows = pl.pallas_call(
        functools.partial(norm_kernel, n_sub),
        out_shape=(
            shape((streams, width), F32),
            shape((streams, width + table_width), BF16),
        ),
        in_specs=[VMEM] * (n_sub + 3) + [HBM] * 2,
        out_specs=(VMEM, VMEM),
        compiler_params=params(8),
        name="norm",
    )(
        *exchange(partial),
        resident,
        norm_gain,
        table,
        in_hbm(expert_up[0]),
        in_hbm(expert_down[0]),
    )
    chips = len(chip_steps)
    rows = pl.pallas_call(
        join_kernel,
        out_shape=shape((chips * streams, width + table_width), BF16),
        in_specs=[VMEM] * chips,
        out_specs=VMEM,
        compiler_params=params(4),
        name="join",
    )(*exchange([rows] * chips, "expert"))
    summed = pl.pallas_call(
        functools.partial(expert_kernel, experts, n_sub),
        out_shape=tuple(shape((chips * streams, width), BF16 if step else F32) for step in steps),
        in_specs=[VMEM] * (n_sub + 6),
        out_specs=(VMEM,) * n_sub,
        compiler_params=params(8 + experts * streams // 64),
        name="expert",
    )(*gather(rows), *(in_vmem(w[0]) for w in (*mine, *twin)))
    summed = pl.pallas_call(
        functools.partial(fold_kernel, n_sub),
        out_shape=tuple(shape((streams, width), BF16 if step else F32) for step in chip_steps),
        in_specs=[VMEM] * n_sub,
        out_specs=(VMEM,) * chips,
        compiler_params=params(8),
        name="fold",
    )(*exchange(summed))
    return pl.pallas_call(
        finish_kernel,
        out_shape=shape((streams, width), BF16),
        in_specs=[VMEM] * (chips + 1),
        out_specs=VMEM,
        compiler_params=params(4),
        name="finish",
    )(hidden, *exchange(summed, "expert"))


def solution(mesh):
    rows = P(("groups", "expert", "sub"), None)
    cache = P(("groups", "expert", "sub"), None, None)
    weights = P(("expert", "sub"), None, None)
    return jax.shard_map(
        body,
        mesh=mesh,
        in_specs=(
            rows,
            rows,
            rows,
            rows,
            cache,
            cache,
            P(("groups", "expert", "sub")),
            P("sub", None),
            P(),
            rows,
            rows,
            weights,
            weights,
            weights,
        ),
        out_specs=rows,
        check_vma=False,
    )
```
